32 devices in a mesh: hid: 4 (over y, x), wid: 4 (over z), rep: 2 (over core).
Axes of the slice: x: 2, y: 2, z: 4, core: 2. Of those that a mesh axis runs over, the one named last changes fastest.
Arguments:
- grad_out: bfloat16 [2, 1024, 8192], P('rep', None, 'wid'), may hold values from -6 to 6
- down_weight: bfloat16 [28672, 8192], P('hid', 'wid'), may hold values from -0.03125 to 0.03125
- saved_gate: bfloat16 [2, 1024, 28672], P('rep', 'wid', 'hid'), may hold values from -6 to 6
- saved_up: bfloat16 [2, 1024, 28672], P('rep', 'wid', 'hid'), may hold values from -6 to 6
- saved_codes: int32 [2, 1024, 28672], P('rep', 'wid', 'hid'), may hold values from -128 to 127, as said below
- exponents: int32 [2, 1024, 224], P('rep', 'wid', 'hid'), may hold values from -12 to -9
Outputs:
- grad_gate: bfloat16 [2, 1024, 28672], P('rep', 'wid', 'hid')
- grad_up: bfloat16 [2, 1024, 28672], P('rep', 'wid', 'hid')
- grad_down: float32 [28672, 8192], P('hid', ('wid', 'rep'))
The draws below stay inside these ranges and needn't reach their ends.
Inputs may be any that keep to these rules, and one draw needn't show every extreme that they name: `saved_codes`: codes at the clip limits -128 and 127 both occur.
All inputs are finite; a program needn't handle non-finite values.
Results may differ from the reference program's by a relative error of at most 0.014.
Values may be sent and summed in bfloat16 or wider, within the bound.
A program may use at most 192 MiB of HBM per device.

```python
import math
import jax
import jax.numpy as jnp
from jax import lax

D = 8192
FF = 28672
BLOCK = 128
REPS = 2
GROUPS = 4
SLICES = 4
GROUP_TOK = 1024


def draw_saved_codes(key, part):
    raw_values = jax.random.randint(key, (REPS, GROUP_TOK, FF), -160, 160, dtype=jnp.int32)
    return jnp.clip(raw_values, -128, 127)


def touch_ends(array, key, least, largest):
    spot = [jax.random.randint(jax.random.fold_in(key, axis), (), 0, length) for axis, length in enumerate(array.shape)]
    longest = array.shape.index(max(array.shape))
    neighbour = spot[:longest] + [(spot[longest] + 1) % array.shape[longest]] + spot[longest + 1:]
    return array.at[tuple(spot)].set(least).at[tuple(neighbour)].set(largest)


def strengthened(values, key, source, target, parts, factor):
    owner, partner = [(jnp.arange(values.shape[dim]) // (values.shape[dim] // parts)).reshape([-1 if axis == dim else 1 for axis in range(values.ndim)]) for dim in (source, target)]
    chosen = jax.random.permutation(key, parts)[partner]
    strong = (owner == chosen) | (owner == (partner + parts // 2) % parts)
    return jnp.where(strong, factor * values, values)


def level_of(stream_key, extent, split, low, high):
    def one(position, shards_of):
        steps = jax.random.uniform(jax.random.fold_in(jax.random.fold_in(stream_key, 6), position), (shards_of,), jnp.float32, low / len(split), high / len(split))
        return jnp.repeat(jnp.exp(steps), extent[position] // shards_of).reshape((-1,) + (1,) * (len(extent) - position - 1))

    level = one(*split[0])
    for cut in split[1:]:
        level = level * one(*cut)
    return level


def gaussian(stream_key, extent, width, bound, shards=(), kind=jnp.bfloat16):
    factor_of = level_of(stream_key, extent, shards, -0.22, 0.18) if shards else 1.0
    result = jax.random.normal(stream_key, extent, jnp.float32) * width * factor_of
    return jnp.minimum(jnp.maximum(result, -bound), bound).astype(kind)


def bell_draw_with(rng, dims, spread, limit, shards, heavy, kind=jnp.bfloat16):
    result = spread * jax.random.normal(rng, dims, jnp.float32)
    if shards:
        result = result * level_of(rng, dims, shards, -0.22, 0.18)
    return jnp.clip(strengthened(result, jax.random.fold_in(rng, 3), *heavy), -limit, limit).astype(kind)


def setup_inputs(seed: int = 0) -> dict:
    seeds = jax.random.split(jax.random.key(seed), 7)
    grad_out = bell_draw_with(seeds[0], (REPS, GROUP_TOK, D), 1.0, 6.0, ((0, 2), (2, 4)), (2, 1, 4, 2.0))
    down_weight = gaussian(seeds[1], (FF, D), FF ** -0.5, 0.03125, ((0, 4), (1, 4)))
    saved_gate = gaussian(seeds[2], (REPS, GROUP_TOK, FF), 1.0, 6.0, ((0, 2), (1, 4), (2, 4)))
    saved_up = gaussian(seeds[3], (REPS, GROUP_TOK, FF), 1.0, 6.0, ((0, 2), (1, 4), (2, 4)))
    saved_codes = draw_saved_codes(jax.random.fold_in(seeds[6], 71), 0)
    exponents = touch_ends(jax.random.randint(seeds[5], (REPS, GROUP_TOK, FF // BLOCK), -12, -8), jax.random.fold_in(seeds[5], 1), -12, (-8) - 1).astype(jnp.int32)
    return {"grad_out": grad_out, "down_weight": down_weight, "saved_gate": saved_gate, "saved_up": saved_up, "saved_codes": saved_codes, "exponents": exponents}


def sylvester(order):
    indices = jnp.arange(order, dtype=jnp.int32)
    both = jnp.bitwise_and(indices[:, None], indices[None, :])
    parity = jnp.zeros((order, order), jnp.int32)
    for bit_index in range(order.bit_length() - 1):
        parity = jnp.bitwise_xor(parity, jnp.bitwise_and(jnp.right_shift(both, bit_index), 1))
    return (1 - 2 * parity).astype(jnp.float32)

def reference(grad_out, down_weight, saved_gate, saved_up, saved_codes, exponents):
    tokens_all = REPS * GROUP_TOK
    out_flat = grad_out.reshape(tokens_all, D)
    codes_flat = saved_codes.reshape(tokens_all, FF)
    scales = jnp.exp2(exponents.reshape(tokens_all, FF // BLOCK).astype(jnp.float32))
    dequant = (codes_flat.astype(jnp.float32).reshape(tokens_all, FF // BLOCK, BLOCK) * scales[:, :, None]).reshape(tokens_all, FF).astype(jnp.bfloat16)
    width_part = D // SLICES
    grad_quant = jnp.zeros((tokens_all, FF), jnp.float32)
    for column_block in range(SLICES):
        lower = column_block * width_part
        partial_sum = lax.dot_general(out_flat[:, lower:lower + width_part], down_weight[:, lower:lower + width_part], (((1,), (1,)), ((), ())), preferred_element_type=jnp.float32)
        grad_quant = grad_quant + lax.optimization_barrier(partial_sum.astype(jnp.bfloat16)).astype(jnp.float32)
    keep_mask = (codes_flat > -128) & (codes_flat < 127)
    masked = jnp.where(keep_mask, grad_quant, jnp.float32(0.0))
    table_block = sylvester(BLOCK) / math.sqrt(BLOCK)
    table_group = sylvester(GROUPS) / math.sqrt(GROUPS)
    shaped = masked.reshape(tokens_all, GROUPS, FF // GROUPS // BLOCK, BLOCK)
    shaped = jnp.einsum('tgbk,kj->tgbj', shaped, table_block, precision=lax.Precision.HIGHEST)
    shaped = jnp.einsum('tgbj,ge->tebj', shaped, table_group, precision=lax.Precision.HIGHEST)
    grad_hidden = shaped.reshape(tokens_all, FF)
    gate_full = saved_gate.reshape(tokens_all, FF).astype(jnp.float32)
    up_full = saved_up.reshape(tokens_all, FF).astype(jnp.float32)
    sigmoid_gate = jax.nn.sigmoid(gate_full)
    grad_gate = (grad_hidden * up_full * sigmoid_gate * (1.0 + gate_full * (1.0 - sigmoid_gate))).astype(jnp.bfloat16)
    grad_up = (grad_hidden * gate_full * sigmoid_gate).astype(jnp.bfloat16)
    grad_down = jnp.zeros((FF, D), jnp.float32)
    for replica in range(REPS):
        lower = replica * GROUP_TOK
        partial_sum = lax.dot_general(dequant[lower:lower + GROUP_TOK], out_flat[lower:lower + GROUP_TOK], (((0,), (0,)), ((), ())), preferred_element_type=jnp.float32)
        grad_down = grad_down + lax.optimization_barrier(partial_sum.astype(jnp.bfloat16)).astype(jnp.float32)
    return (grad_gate.reshape(REPS, GROUP_TOK, FF), grad_up.reshape(REPS, GROUP_TOK, FF), grad_down)
```

```python
import functools
import math

import jax
import jax.numpy as jnp
from jax import lax
from jax.experimental import pallas as pl
from jax.experimental.pallas import tpu as pltpu
from jax.sharding import PartitionSpec as P

BLOCK = 128
GROUPS = 4
F32 = jnp.float32
BF16 = jnp.bfloat16


def sylvester(order):
    indices = jnp.arange(order, dtype=jnp.int32)
    both = jnp.bitwise_and(indices[:, None], indices[None, :])
    parity = jnp.zeros((order, order), jnp.int32)
    for bit_index in range(order.bit_length() - 1):
        parity = jnp.bitwise_xor(parity, jnp.bitwise_and(jnp.right_shift(both, bit_index), 1))
    return (1 - 2 * parity).astype(F32)


def dequant_kernel(codes_ref, scales_ref, *outs):
    per_part = outs[0].shape[1] // BLOCK
    for part, out in enumerate(outs):
        for b in range(per_part):
            at = part * per_part + b
            code = codes_ref[:, at * BLOCK:(at + 1) * BLOCK].astype(F32)
            out[:, b * BLOCK:(b + 1) * BLOCK] = (code * scales_ref[:, at:at + 1]).astype(BF16)


def dequantize(codes, scales, parts):
    tok, hidden = codes.shape
    tile = min(tok, 64)
    width = hidden // parts
    return pl.pallas_call(
        dequant_kernel,
        grid=(tok // tile,),
        in_specs=[
            pl.BlockSpec((tile, hidden), lambda i: (i, 0)),
            pl.BlockSpec((tile, scales.shape[1]), lambda i: (i, 0)),
        ],
        out_specs=[pl.BlockSpec((tile, width), lambda i: (i, 0))] * parts,
        out_shape=[jax.ShapeDtypeStruct((tok, width), BF16)] * parts,
        cost_estimate=pl.CostEstimate(
            flops=tok * hidden, bytes_accessed=6 * tok * hidden, transcendentals=0
        ),
    )(codes, scales)


def rotate_kernel(own_ref, right_ref, left_ref, codes_ref, table_ref, out_ref):
    table = table_ref[...]
    for b in range(out_ref.shape[1] // BLOCK):
        at = slice(b * BLOCK, (b + 1) * BLOCK)
        total = own_ref[:, at].astype(F32) + right_ref[:, at].astype(F32) + left_ref[:, at].astype(F32)
        code = codes_ref[:, at]
        masked = jnp.where((code > -128) & (code < 127), total, 0.0).astype(BF16)
        mixed = jnp.dot(masked, table, preferred_element_type=F32)
        out_ref[:, at] = (mixed * (1.0 / math.sqrt(BLOCK * GROUPS))).astype(BF16)


def rotate(own, right, left, codes, table, part):
    tok, width = own.shape
    tile = min(tok, 128)
    spec = pl.BlockSpec((tile, width), lambda i: (i, 0))
    return pl.pallas_call(
        rotate_kernel,
        grid=(tok // tile,),
        in_specs=[
            spec,
            spec,
            spec,
            pl.BlockSpec((tile, width), lambda i: (i, part)),
            pl.BlockSpec((BLOCK, BLOCK), lambda i: (0, 0)),
        ],
        out_specs=spec,
        out_shape=jax.ShapeDtypeStruct((tok, width), BF16),
        cost_estimate=pl.CostEstimate(
            flops=2 * BLOCK * tok * width, bytes_accessed=12 * tok * width, transcendentals=0
        ),
    )(own, right, left, codes, table)


def gate_kernel(first, sign_ref, own_ref, other_ref, gate_ref, up_ref, *refs):
    gate_out, up_out = refs if first else refs[2:]
    hidden = other_ref[...].astype(F32) + sign_ref[0, 0] * own_ref[...].astype(F32)
    gate = gate_ref[...].astype(F32)
    up = up_ref[...].astype(F32)
    s = jax.nn.sigmoid(gate)
    gate_out[...] = (hidden * up * s * (1.0 + gate * (1.0 - s))).astype(BF16)
    up_out[...] = (hidden * gate * s).astype(BF16)


def gate_grads(sign, own, other, gate, up, part, earlier):
    tok, width = own.shape
    tile = min(tok, 64)
    spec = pl.BlockSpec((tile, width), lambda i: (i, 0))
    at_part = pl.BlockSpec((tile, width), lambda i: (i, part))
    held = [] if earlier is None else list(earlier)
    return pl.pallas_call(
        functools.partial(gate_kernel, earlier is None),
        grid=(tok // tile,),
        in_specs=[pl.BlockSpec(memory_space=pltpu.SMEM), spec, spec, at_part, at_part]
        + [pl.BlockSpec(memory_space=pl.ANY)] * len(held),
        out_specs=[at_part, at_part],
        out_shape=[jax.ShapeDtypeStruct(gate.shape, BF16)] * 2,
        input_output_aliases={5: 0, 6: 1} if held else {},
        cost_estimate=pl.CostEstimate(
            flops=10 * tok * width, bytes_accessed=12 * tok * width, transcendentals=tok * width
        ),
    )(sign, own, other, gate, up, *held)


def shards(grad_out, down_weight, saved_gate, saved_up, saved_codes, exponents):
    rows = grad_out[0]
    codes, gate, up = saved_codes[0], saved_gate[0], saved_up[0]
    tok, hidden = codes.shape
    n = lax.axis_size("wid")
    me = lax.axis_index("wid")
    hid_size = lax.axis_size("hid")
    reps = lax.axis_size("rep")
    blocks = hidden // BLOCK
    parts = 4 if blocks % 4 == 0 else 2 if blocks % 2 == 0 else 1
    width = hidden // parts
    scales = jnp.exp2(exponents[0].astype(F32))
    dequant = dequantize(codes, scales, parts)

    chunk = lambda array, at: lax.dynamic_slice_in_dim(array, lax.rem(at + n, n) * tok, tok, 0)
    turned = jnp.concatenate([chunk(rows, me - c) for c in range(n)], axis=0)
    every = lax.all_gather(turned, "rep", axis=0, tiled=True)
    columns = rows.shape[1] // reps
    go_columns = lax.dynamic_slice_in_dim(every, lax.axis_index("rep") * columns, columns, 1)

    table = sylvester(BLOCK).astype(BF16)
    to_right = [(i, i + 1) for i in range(n - 1)]
    to_left = [(i + 1, i) for i in range(n - 1)]
    step = hid_size // GROUPS
    group = lax.axis_index("hid") // step
    bits = GROUPS.bit_length() - 1

    def exchange(array, bit):
        return lax.ppermute(array, "hid", [(h, h ^ (step << bit)) for h in range(hid_size)])

    def sign_of(bit):
        return jnp.where((group >> bit) & 1 == 0, 1.0, -1.0).astype(F32)

    grads = None
    grad_down = jnp.zeros((hidden, columns), F32)
    for part in range(parts):
        weight = lax.slice_in_dim(down_weight, part * width, (part + 1) * width, axis=0)
        partial = lax.dot_general(
            rows, weight, (((1,), (1,)), ((), ())), preferred_element_type=F32
        ).astype(BF16)
        right = left = dequant[part]
        rights, lefts = [], []
        back = n - 1 - me
        for slot in range(n):
            if slot:
                add_r = jnp.where(slot <= me, 0.0, chunk(partial, me - slot).astype(F32))
                right = (rights[-1].astype(F32) + add_r).astype(BF16)
                add_l = jnp.where(slot <= back, 0.0, chunk(partial, me + slot).astype(F32))
                left = (lefts[-1].astype(F32) + add_l).astype(BF16)
            rights.append(lax.ppermute(right, "wid", to_right))
            lefts.append(lax.ppermute(left, "wid", to_left))
        arrived = [jnp.where(me > s, rights[s], lefts[n - 2 - s]) for s in range(n - 1)]
        gathered = jnp.concatenate([dequant[part]] + arrived, axis=0)
        both = lax.all_gather(gathered, "rep", axis=0, tiled=True)
        term = lax.dot_general(both, go_columns, (((0,), (0,)), ((), ())), preferred_element_type=F32)
        grad_down = lax.dynamic_update_slice_in_dim(grad_down, term, part * width, 0)

        mixed = rotate(chunk(partial, me), rights[-1], lefts[-1], codes, table, part)
        order = [(part + k) % bits for k in range(bits)]
        for bit in order[:-1]:
            other = exchange(mixed, bit)
            mixed = (other.astype(F32) + sign_of(bit) * mixed.astype(F32)).astype(BF16)
        other = exchange(mixed, order[-1])
        sign = sign_of(order[-1]).reshape(1, 1)
        grads = gate_grads(sign, mixed, other, gate, up, part, grads)
    return (grads[0][None], grads[1][None], grad_down)


def solution(mesh):
    in_specs = (
        P("rep", None, "wid"),
        P("hid", "wid"),
        P("rep", "wid", "hid"),
        P("rep", "wid", "hid"),
        P("rep", "wid", "hid"),
        P("rep", "wid", "hid"),
    )
    out_specs = (P("rep", "wid", "hid"), P("rep", "wid", "hid"), P("hid", ("wid", "rep")))
    return jax.shard_map(shards, mesh=mesh, in_specs=in_specs, out_specs=out_specs, check_vma=False)
```

```python
import functools
import math

import jax
import jax.numpy as jnp
from jax import lax
from jax.experimental import pallas as pl
from jax.experimental.pallas import tpu as pltpu
from jax.sharding import PartitionSpec as P

BLOCK = 128
GROUPS = 4
F32 = jnp.float32
BF16 = jnp.bfloat16


def sylvester(order):
    indices = jnp.arange(order, dtype=jnp.int32)
    both = jnp.bitwise_and(indices[:, None], indices[None, :])
    parity = jnp.zeros((order, order), jnp.int32)
    for bit_index in range(order.bit_length() - 1):
        parity = jnp.bitwise_xor(parity, jnp.bitwise_and(jnp.right_shift(both, bit_index), 1))
    return (1 - 2 * parity).astype(F32)


def dequant_kernel(part, codes_ref, scales_ref, out):
    per_part = out.shape[1] // BLOCK
    for b in range(per_part):
        at = part * per_part + b
        code = codes_ref[:, b * BLOCK:(b + 1) * BLOCK].astype(F32)
        out[:, b * BLOCK:(b + 1) * BLOCK] = (code * scales_ref[:, at:at + 1]).astype(BF16)


def dequantize(codes, scales, part, parts):
    tok, hidden = codes.shape
    tile = min(tok, 64)
    width = hidden // parts
    return pl.pallas_call(
        functools.partial(dequant_kernel, part),
        grid=(tok // tile,),
        in_specs=[
            pl.BlockSpec((tile, width), lambda i: (i, part)),
            pl.BlockSpec((tile, scales.shape[1]), lambda i: (i, 0)),
        ],
        out_specs=pl.BlockSpec((tile, width), lambda i: (i, 0)),
        out_shape=jax.ShapeDtypeStruct((tok, width), BF16),
        cost_estimate=pl.CostEstimate(
            flops=tok * width, bytes_accessed=6 * tok * width, transcendentals=0
        ),
    )(codes, scales)


def blank_kernel(out_ref):
    pass


def blank(shape, dtype):
    return pl.pallas_call(
        blank_kernel,
        out_specs=pl.BlockSpec(memory_space=pl.ANY),
        out_shape=jax.ShapeDtypeStruct(shape, dtype),
        cost_estimate=pl.CostEstimate(flops=0, bytes_accessed=0, transcendentals=0),
    )()


def rotate_kernel(own_ref, right_ref, left_ref, codes_ref, table_ref, out_ref):
    table = table_ref[...]
    for b in range(out_ref.shape[1] // BLOCK):
        at = slice(b * BLOCK, (b + 1) * BLOCK)
        total = own_ref[:, at].astype(F32) + right_ref[:, at].astype(F32) + left_ref[:, at].astype(F32)
        code = codes_ref[:, at]
        masked = jnp.where((code > -128) & (code < 127), total, 0.0).astype(BF16)
        mixed = jnp.dot(masked, table, preferred_element_type=F32)
        out_ref[:, at] = (mixed * (1.0 / math.sqrt(BLOCK * GROUPS))).astype(BF16)


def rotate(own, right, left, codes, table, part):
    tok, width = own.shape
    tile = min(tok, 128)
    spec = pl.BlockSpec((tile, width), lambda i: (i, 0))
    return pl.pallas_call(
        rotate_kernel,
        grid=(tok // tile,),
        in_specs=[
            spec,
            spec,
            spec,
            pl.BlockSpec((tile, width), lambda i: (i, part)),
            pl.BlockSpec((BLOCK, BLOCK), lambda i: (0, 0)),
        ],
        out_specs=spec,
        out_shape=jax.ShapeDtypeStruct((tok, width), BF16),
        cost_estimate=pl.CostEstimate(
            flops=2 * BLOCK * tok * width, bytes_accessed=12 * tok * width, transcendentals=0
        ),
    )(own, right, left, codes, table)


def gate_kernel(first, sign_ref, own_ref, other_ref, gate_ref, up_ref, *refs):
    gate_out, up_out = refs if first else refs[2:]
    hidden = other_ref[...].astype(F32) + sign_ref[0, 0] * own_ref[...].astype(F32)
    gate = gate_ref[...].astype(F32)
    up = up_ref[...].astype(F32)
    s = jax.nn.sigmoid(gate)
    gate_out[...] = (hidden * up * s * (1.0 + gate * (1.0 - s))).astype(BF16)
    up_out[...] = (hidden * gate * s).astype(BF16)


def gate_grads(sign, own, other, gate, up, part, earlier):
    tok, width = own.shape
    tile = min(tok, 64)
    spec = pl.BlockSpec((tile, width), lambda i: (i, 0))
    at_part = pl.BlockSpec((tile, width), lambda i: (i, part))
    held = [] if earlier is None else list(earlier)
    return pl.pallas_call(
        functools.partial(gate_kernel, earlier is None),
        grid=(tok // tile,),
        in_specs=[pl.BlockSpec(memory_space=pltpu.SMEM), spec, spec, at_part, at_part]
        + [pl.BlockSpec(memory_space=pl.ANY)] * len(held),
        out_specs=[at_part, at_part],
        out_shape=[jax.ShapeDtypeStruct(gate.shape, BF16)] * 2,
        input_output_aliases={5: 0, 6: 1} if held else {},
        cost_estimate=pl.CostEstimate(
            flops=10 * tok * width, bytes_accessed=12 * tok * width, transcendentals=tok * width
        ),
    )(sign, own, other, gate, up, *held)


def shards(grad_out, down_weight, saved_gate, saved_up, saved_codes, exponents):
    rows = grad_out[0]
    codes, gate, up = saved_codes[0], saved_gate[0], saved_up[0]
    tok, hidden = codes.shape
    n = lax.axis_size("wid")
    me = lax.axis_index("wid")
    hid_size = lax.axis_size("hid")
    reps = lax.axis_size("rep")
    blocks = hidden // BLOCK
    parts = 4 if blocks % 4 == 0 else 2 if blocks % 2 == 0 else 1
    width = hidden // parts
    scales = jnp.exp2(exponents[0].astype(F32))
    dequant = [dequantize(codes, scales, part, parts) for part in range(parts)]
    tie = lax.optimization_barrier

    chunk = lambda array, at: lax.dynamic_slice_in_dim(array, lax.rem(at + n, n) * tok, tok, 0)
    later_rows, dequant[0] = tie((rows, dequant[0]))
    turned = jnp.concatenate([chunk(later_rows, me - c) for c in range(n)], axis=0)
    every = lax.all_gather(turned, "rep", axis=0, tiled=True)
    columns = rows.shape[1] // reps
    go_columns = lax.dynamic_slice_in_dim(every, lax.axis_index("rep") * columns, columns, 1)

    table = sylvester(BLOCK).astype(BF16)
    to_right = [(i, i + 1) for i in range(n - 1)]
    to_left = [(i + 1, i) for i in range(n - 1)]
    step = hid_size // GROUPS
    group = lax.axis_index("hid") // step
    bits = GROUPS.bit_length() - 1
    back = n - 1 - me

    def exchange(array, bit):
        return lax.ppermute(array, "hid", [(h, h ^ (step << bit)) for h in range(hid_size)])

    def sign_of(bit):
        return jnp.where((group >> bit) & 1 == 0, 1.0, -1.0).astype(F32)

    def product(part):
        weight = lax.slice_in_dim(down_weight, part * width, (part + 1) * width, axis=0)
        return lax.dot_general(
            rows, weight, (((1,), (1,)), ((), ())), preferred_element_type=F32
        ).astype(BF16)

    def weight_grad(part):
        term = lax.dot_general(
            held["both", part], go_columns, (((0,), (0,)), ((), ())), preferred_element_type=F32
        )
        return lax.dynamic_update_slice_in_dim(held["down"], term, part * width, 0)

    def order(part):
        return [(part + k) % bits for k in range(bits)]

    def mix(part, k):
        bit = order(part)[k]
        mixed = held["mixed", part]
        other = exchange(mixed, bit)
        if part in beside:
            beside.remove(part)
            mixed, held["down"] = tie((mixed, weight_grad(part)))
        return (other.astype(F32) + sign_of(bit) * mixed.astype(F32)).astype(BF16)

    def finish(part):
        bit = order(part)[-1]
        other = exchange(held["mixed", part], bit)
        return gate_grads(
            sign_of(bit).reshape(1, 1), held["mixed", part], other, gate, up, part, held["grads"]
        )

    chains = 2 if parts % 2 == 0 else 1
    steps = [
        (turn * chains + chain, slot)
        for turn in range(parts // chains)
        for slot in range(n)
        for chain in range(chains)
    ]
    tasks = []
    for part in range(parts):
        first = (part // chains) * n * chains + part % chains
        last = first + (n - 1) * chains
        ready = first if part < chains else first - (n - 1) * chains + 1
        tasks.append((ready, "product", part))
        tasks.append((last + 3, "weight", part))
        tasks.append((last + 3, "rotate", part))
        for k in range(bits - 1):
            tasks.append((last + 5 + 2 * k, "mix%d" % k, part))
        tasks.append((last + 5 + 2 * (bits - 1), "finish", part))
    tasks = sorted(tasks, key=lambda task: (task[0], task[2]))

    held = {"grads": None, "down": blank((hidden, columns), F32)}
    rights, lefts = {}, {}
    beside = []

    def run(kind, part):
        if kind == "product":
            held["partial", part] = product(part)
            return "partial", part
        if kind == "weight":
            held["down"] = weight_grad(part)
            return "down"
        if kind == "rotate":
            held["mixed", part] = rotate(
                chunk(held["partial", part], me), rights[part], lefts[part], codes, table, part
            )
            return "mixed", part
        if kind == "finish":
            held["grads"] = finish(part)
            return "grads"
        held["mixed", part] = mix(part, int(kind[3:]))
        return "mixed", part

    moved = {}
    for at, (part, slot) in enumerate(steps):
        if slot == 0:
            right = left = dequant[part]
        else:
            partial = held["partial", part]
            add_r = jnp.where(slot <= me, 0.0, chunk(partial, me - slot).astype(F32))
            right = (moved[part, slot - 1][0].astype(F32) + add_r).astype(BF16)
            add_l = jnp.where(slot <= back, 0.0, chunk(partial, me + slot).astype(F32))
            left = (moved[part, slot - 1][1].astype(F32) + add_l).astype(BF16)
        keys = [run(kind, which) for when, kind, which in tasks if when == at - 1]
        keys = list(dict.fromkeys(keys))
        previous = steps[at - chains] if at >= chains else None
        waits = [held[key] for key in keys]
        extra = moved[previous] if previous and slot == 0 else None
        (right, left), waits, extra = tie(((right, left), waits, extra))
        for key, value in zip(keys, waits):
            held[key] = value
        if extra is not None:
            moved[previous] = extra
            rights[previous[0]], lefts[previous[0]] = extra
        moved[part, slot] = (
            lax.ppermute(right, "wid", to_right), lax.ppermute(left, "wid", to_left)
        )
        if slot == n - 1:
            rights[part], lefts[part] = moved[part, slot]
        if slot == n - 1 or n == 1:
            arrived = [
                jnp.where(me > s, moved[part, s][0], moved[part, n - 2 - s][1]) for s in range(n - 1)
            ]
            gathered = jnp.concatenate([dequant[part]] + arrived, axis=0)
            held["both", part] = lax.all_gather(gathered, "rep", axis=0, tiled=True)
    rest = [(kind, part) for when, kind, part in tasks if when >= len(steps) - 1]
    beside += [part for kind, part in rest if kind == "weight" and ("mix0", part) in rest]
    for kind, part in rest:
        if kind != "weight" or part not in beside:
            run(kind, part)
    grads, grad_down = held["grads"], held["down"]
    return (grads[0][None], grads[1][None], grad_down)


def solution(mesh):
    in_specs = (
        P("rep", None, "wid"),
        P("hid", "wid"),
        P("rep", "wid", "hid"),
        P("rep", "wid", "hid"),
        P("rep", "wid", "hid"),
        P("rep", "wid", "hid"),
    )
    out_specs = (P("rep", "wid", "hid"), P("rep", "wid", "hid"), P("hid", ("wid", "rep")))
    return jax.shard_map(shards, mesh=mesh, in_specs=in_specs, out_specs=out_specs, check_vma=False)
```

```python
import functools
import math

import jax
import jax.numpy as jnp
from jax import lax
from jax.experimental import pallas as pl
from jax.experimental.pallas import tpu as pltpu
from jax.sharding import PartitionSpec as P

BLOCK = 128
GROUPS = 4
F32 = jnp.float32
BF16 = jnp.bfloat16


def sylvester(order):
    indices = jnp.arange(order, dtype=jnp.int32)
    both = jnp.bitwise_and(indices[:, None], indices[None, :])
    parity = jnp.zeros((order, order), jnp.int32)
    for bit_index in range(order.bit_length() - 1):
        parity = jnp.bitwise_xor(parity, jnp.bitwise_and(jnp.right_shift(both, bit_index), 1))
    return (1 - 2 * parity).astype(F32)


def dequant_kernel(part, codes_ref, scales_ref, out):
    per_part = out.shape[1] // BLOCK
    for b in range(per_part):
        at = part * per_part + b
        code = codes_ref[:, b * BLOCK:(b + 1) * BLOCK].astype(F32)
        out[:, b * BLOCK:(b + 1) * BLOCK] = (code * scales_ref[:, at:at + 1]).astype(BF16)


def dequantize(codes, scales, part, parts):
    tok, hidden = codes.shape
    tile = min(tok, 64)
    width = hidden // parts
    return pl.pallas_call(
        functools.partial(dequant_kernel, part),
        grid=(tok // tile,),
        in_specs=[
            pl.BlockSpec((tile, width), lambda i: (i, part)),
            pl.BlockSpec((tile, scales.shape[1]), lambda i: (i, 0)),
        ],
        out_specs=pl.BlockSpec((tile, width), lambda i: (i, 0)),
        out_shape=jax.ShapeDtypeStruct((tok, width), BF16),
        cost_estimate=pl.CostEstimate(
            flops=tok * width, bytes_accessed=6 * tok * width, transcendentals=0
        ),
    )(codes, scales)


def blank_kernel(out_ref):
    pass


def blank(shape, dtype):
    return pl.pallas_call(
        blank_kernel,
        out_specs=pl.BlockSpec(memory_space=pl.ANY),
        out_shape=jax.ShapeDtypeStruct(shape, dtype),
        cost_estimate=pl.CostEstimate(flops=0, bytes_accessed=0, transcendentals=0),
    )()


def rotate_kernel(own_ref, right_ref, left_ref, codes_ref, table_ref, out_ref):
    table = table_ref[...]
    for b in range(out_ref.shape[1] // BLOCK):
        at = slice(b * BLOCK, (b + 1) * BLOCK)
        total = own_ref[:, at].astype(F32) + right_ref[:, at].astype(F32) + left_ref[:, at].astype(F32)
        code = codes_ref[:, at]
        masked = jnp.where((code > -128) & (code < 127), total, 0.0).astype(BF16)
        mixed = jnp.dot(masked, table, preferred_element_type=F32)
        out_ref[:, at] = (mixed * (1.0 / math.sqrt(BLOCK * GROUPS))).astype(BF16)


def rotate(own, right, left, codes, table, part):
    tok, width = own.shape
    tile = min(tok, 128)
    spec = pl.BlockSpec((tile, width), lambda i: (i, 0))
    return pl.pallas_call(
        rotate_kernel,
        grid=(tok // tile,),
        in_specs=[
            spec,
            spec,
            spec,
            pl.BlockSpec((tile, width), lambda i: (i, part)),
            pl.BlockSpec((BLOCK, BLOCK), lambda i: (0, 0)),
        ],
        out_specs=spec,
        out_shape=jax.ShapeDtypeStruct((tok, width), BF16),
        cost_estimate=pl.CostEstimate(
            flops=2 * BLOCK * tok * width, bytes_accessed=12 * tok * width, transcendentals=0
        ),
    )(own, right, left, codes, table)


def gate_kernel(first, sign_ref, own_ref, other_ref, gate_ref, up_ref, *refs):
    gate_out, up_out = refs if first else refs[2:]
    hidden = other_ref[...].astype(F32) + sign_ref[0, 0] * own_ref[...].astype(F32)
    gate = gate_ref[...].astype(F32)
    up = up_ref[...].astype(F32)
    s = jax.nn.sigmoid(gate)
    gate_out[...] = (hidden * up * s * (1.0 + gate * (1.0 - s))).astype(BF16)
    up_out[...] = (hidden * gate * s).astype(BF16)


def gate_grads(sign, own, other, gate, up, part, earlier):
    tok, width = own.shape
    tile = min(tok, 64)
    spec = pl.BlockSpec((tile, width), lambda i: (i, 0))
    at_part = pl.BlockSpec((tile, width), lambda i: (i, part))
    held = [] if earlier is None else list(earlier)
    return pl.pallas_call(
        functools.partial(gate_kernel, earlier is None),
        grid=(tok // tile,),
        in_specs=[pl.BlockSpec(memory_space=pltpu.SMEM), spec, spec, at_part, at_part]
        + [pl.BlockSpec(memory_space=pl.ANY)] * len(held),
        out_specs=[at_part, at_part],
        out_shape=[jax.ShapeDtypeStruct(gate.shape, BF16)] * 2,
        input_output_aliases={5: 0, 6: 1} if held else {},
        cost_estimate=pl.CostEstimate(
            flops=10 * tok * width, bytes_accessed=12 * tok * width, transcendentals=tok * width
        ),
    )(sign, own, other, gate, up, *held)


def shards(grad_out, down_weight, saved_gate, saved_up, saved_codes, exponents):
    rows = grad_out[0]
    codes, gate, up = saved_codes[0], saved_gate[0], saved_up[0]
    tok, hidden = codes.shape
    n = lax.axis_size("wid")
    me = lax.axis_index("wid")
    hid_size = lax.axis_size("hid")
    reps = lax.axis_size("rep")
    blocks = hidden // BLOCK
    parts = 4 if blocks % 4 == 0 else 2 if blocks % 2 == 0 else 1
    width = hidden // parts
    scales = jnp.exp2(exponents[0].astype(F32))
    dequant = [dequantize(codes, scales, part, parts) for part in range(parts)]
    tie = lax.optimization_barrier
    chains = 2 if parts % 2 == 0 else 1

    chunk = lambda array, at: lax.dynamic_slice_in_dim(array, lax.rem(at + n, n) * tok, tok, 0)
    rows, dequant[:chains] = tie((rows, dequant[:chains]))
    later_rows = rows
    turned = jnp.concatenate([chunk(later_rows, me - c) for c in range(n)], axis=0)
    every = lax.all_gather(turned, "rep", axis=0, tiled=True)
    columns = rows.shape[1] // reps
    go_columns = lax.dynamic_slice_in_dim(every, lax.axis_index("rep") * columns, columns, 1)

    table = sylvester(BLOCK).astype(BF16)
    to_right = [(i, i + 1) for i in range(n - 1)]
    to_left = [(i + 1, i) for i in range(n - 1)]
    step = hid_size // GROUPS
    group = lax.axis_index("hid") // step
    bits = GROUPS.bit_length() - 1
    back = n - 1 - me

    def exchange(array, bit):
        return lax.ppermute(array, "hid", [(h, h ^ (step << bit)) for h in range(hid_size)])

    def sign_of(bit):
        return jnp.where((group >> bit) & 1 == 0, 1.0, -1.0).astype(F32)

    def product(part):
        weight = lax.slice_in_dim(down_weight, part * width, (part + 1) * width, axis=0)
        return lax.dot_general(
            rows, weight, (((1,), (1,)), ((), ())), preferred_element_type=F32
        ).astype(BF16)

    def weight_grad(part):
        term = lax.dot_general(
            held["both", part], go_columns, (((0,), (0,)), ((), ())), preferred_element_type=F32
        )
        return lax.dynamic_update_slice_in_dim(held["down"], term, part * width, 0)

    def order(part):
        return [(part + k) % bits for k in range(bits)]

    def mix(part, k):
        bit = order(part)[k]
        mixed = held["mixed", part]
        other = exchange(mixed, bit)
        if part in beside:
            beside.remove(part)
            mixed, held["down"] = tie((mixed, weight_grad(part)))
        return (other.astype(F32) + sign_of(bit) * mixed.astype(F32)).astype(BF16)

    def finish(part):
        bit = order(part)[-1]
        other = exchange(held["mixed", part], bit)
        return gate_grads(
            sign_of(bit).reshape(1, 1), held["mixed", part], other, gate, up, part, held["grads"]
        )

    steps = [
        (turn * chains + chain, slot)
        for turn in range(parts // chains)
        for slot in range(n)
        for chain in range(chains)
    ]
    tasks = []
    for part in range(parts):
        first = (part // chains) * n * chains + part % chains
        last = first + (n - 1) * chains
        ready = first if part < chains else first - (n - 1) * chains + 1
        tasks.append((ready, "product", part))
        tasks.append((last + 3, "weight", part))
        tasks.append((last + 3, "rotate", part))
        for k in range(bits - 1):
            tasks.append((last + 5 + 2 * k, "mix%d" % k, part))
        tasks.append((last + 5 + 2 * (bits - 1), "finish", part))
    tasks = sorted(tasks, key=lambda task: (task[0], task[2]))

    held = {"grads": None, "down": blank((hidden, columns), F32)}
    rights, lefts = {}, {}
    beside = []

    def run(kind, part):
        if kind == "product":
            held["partial", part] = product(part)
            return "partial", part
        if kind == "weight":
            held["down"] = weight_grad(part)
            return "down"
        if kind == "rotate":
            held["mixed", part] = rotate(
                chunk(held["partial", part], me), rights[part], lefts[part], codes, table, part
            )
            return "mixed", part
        if kind == "finish":
            held["grads"] = finish(part)
            return "grads"
        held["mixed", part] = mix(part, int(kind[3:]))
        return "mixed", part

    moved = {}
    for at, (part, slot) in enumerate(steps):
        if slot == 0:
            right = left = dequant[part]
        else:
            partial = held["partial", part]
            add_r = jnp.where(slot <= me, 0.0, chunk(partial, me - slot).astype(F32))
            right = (moved[part, slot - 1][0].astype(F32) + add_r).astype(BF16)
            add_l = jnp.where(slot <= back, 0.0, chunk(partial, me + slot).astype(F32))
            left = (moved[part, slot - 1][1].astype(F32) + add_l).astype(BF16)
        keys = [run(kind, which) for when, kind, which in tasks if when == at - 1]
        keys = list(dict.fromkeys(keys))
        previous = steps[at - chains] if at >= chains else None
        keys = [key for key in keys if key[0] != "partial" or key[1] >= chains]
        waits = [held[key] for key in keys]
        extra = moved[previous] if previous and slot == 0 else None
        (right, left), waits, extra = tie(((right, left), waits, extra))
        for key, value in zip(keys, waits):
            held[key] = value
        if extra is not None:
            moved[previous] = extra
            rights[previous[0]], lefts[previous[0]] = extra
        moved[part, slot] = (
            lax.ppermute(right, "wid", to_right), lax.ppermute(left, "wid", to_left)
        )
        if slot == n - 1:
            rights[part], lefts[part] = moved[part, slot]
        if slot == n - 1 or n == 1:
            arrived = [
                jnp.where(me > s, moved[part, s][0], moved[part, n - 2 - s][1]) for s in range(n - 1)
            ]
            gathered = jnp.concatenate([dequant[part]] + arrived, axis=0)
            held["both", part] = lax.all_gather(gathered, "rep", axis=0, tiled=True)
    rest = [(kind, part) for when, kind, part in tasks if when >= len(steps) - 1]
    beside += [part for kind, part in rest if kind == "weight" and ("mix0", part) in rest]
    for kind, part in rest:
        if kind != "weight" or part not in beside:
            run(kind, part)
    grads, grad_down = held["grads"], held["down"]
    return (grads[0][None], grads[1][None], grad_down)


def solution(mesh):
    in_specs = (
        P("rep", None, "wid"),
        P("hid", "wid"),
        P("rep", "wid", "hid"),
        P("rep", "wid", "hid"),
        P("rep", "wid", "hid"),
        P("rep", "wid", "hid"),
    )
    out_specs = (P("rep", "wid", "hid"), P("rep", "wid", "hid"), P("hid", ("wid", "rep")))
    return jax.shard_map(shards, mesh=mesh, in_specs=in_specs, out_specs=out_specs, check_vma=False)
```
